32 devices in a mesh: group: 4 (over y, x), fsdp: 8 (over z, core).
Axes of the slice: x: 2, y: 2, z: 4, core: 2. Of those that a mesh axis runs over, the one named last changes fastest.
Arguments:
- tokens_in: bfloat16 [32768, 2048], P(('group', 'fsdp')), may hold values from -6 to 6
- out_grad: bfloat16 [32768, 2048], P(('group', 'fsdp')), may hold values from -0.59765625 to 0.59765625
- w_in: bfloat16 [4, 2048, 8192], P('group', None, 'fsdp'), may hold values from -0.125 to 0.125
- w_out: bfloat16 [4, 8192, 2048], P('group', 'fsdp'), may hold values from -0.0625 to 0.0625
- chosen: int32 [32, 4, 16], P(('group', 'fsdp')), may hold values from 0 to 1023, as said below
- counts: int32 [32, 4], P(('group', 'fsdp')), may hold values from 1 to 16, as said below
- gates: float32 [32, 4, 16], P(('group', 'fsdp')), may hold values from 0.05 to 1
Outputs:
- grad_in: bfloat16 [32768, 2048], P(('group', 'fsdp'))
- grad_w_in: float32 [4, 2048, 8192], P('group', None, 'fsdp')
- grad_w_out: float32 [4, 8192, 2048], P('group', 'fsdp')
The draws below stay inside these ranges and needn't reach their ends.
Inputs may be any that keep to these rules, and one draw needn't show every extreme that they name: `chosen`: the 16 slots of one image and one expert name distinct positions. `counts`: each image fills all 16 slots of at least one expert.
All inputs are finite; a program needn't handle non-finite values.
Results may differ from the reference program's by a relative error of at most 0.0057.
Values may be sent and summed in bfloat16 or wider, within the bound.
No kernel may reach another device: no remote copies, remote signals or barrier semaphores. Data moves between devices by JAX's collectives and lax.ppermute only.
A program may use at most 128 MiB of HBM per device.

```python
import math
import jax
import jax.numpy as jnp
from jax import lax

D = 2048
FF = 8192
LEN = 1024
CAP = 16
E_WIN = 4
IMAGES = 32
TOKENS = 32768


def draw_counts(key, part):
    count_key, pick_key = jax.random.split(jax.random.fold_in(key, 11))
    base_count = jax.random.randint(count_key, (IMAGES, E_WIN), max(1, CAP // 4), CAP + 1)
    full_expert = jax.random.randint(pick_key, (IMAGES, 1), 0, E_WIN)
    columns = lax.broadcasted_iota(jnp.int32, (IMAGES, E_WIN), 1)
    return jnp.where(columns == full_expert, CAP, base_count).astype(jnp.int32)


def draw_chosen(key, part):
    score_key = jax.random.fold_in(key, 23)
    scores = jax.random.randint(score_key, (IMAGES, E_WIN, LEN), 0, 2 ** 30 // LEN) * LEN
    scores = scores + lax.broadcasted_iota(jnp.int32, (IMAGES, E_WIN, LEN), 2)
    return lax.top_k(scores, CAP)[1].astype(jnp.int32)


def level_of(key, dims, shards, low, top_value):
    def one(dim, shards_of):
        draws = jax.random.uniform(jax.random.fold_in(jax.random.fold_in(key, 6), dim), (shards_of,), jnp.float32, low / len(shards), top_value / len(shards))
        return jnp.repeat(jnp.exp(draws), dims[dim] // shards_of).reshape((-1,) + (1,) * (len(dims) - dim - 1))

    level = one(*shards[0])
    for cut in shards[1:]:
        level = level * one(*cut)
    return level


def bell_draw(stream_key, extent, width, reach, shards=(), kind=jnp.bfloat16):
    values = width * jax.random.normal(stream_key, extent, jnp.float32)
    if shards:
        values = values * level_of(stream_key, extent, shards, -0.22, 0.18)
    return jnp.clip(values, -reach, reach).astype(kind)


def setup_inputs(seed: int = 0) -> dict:
    seeds = jax.random.split(jax.random.key(seed), 8)
    tokens_in = bell_draw(seeds[0], (TOKENS, D), 1.0, 6.0, ((0, 32),))
    out_grad = bell_draw(seeds[1], (TOKENS, D), 0.1, 0.59765625, ((0, 32),))
    w_in = bell_draw(seeds[2], (E_WIN, D, FF), D ** -0.5, 0.125, ((0, 4), (2, 8)))
    w_out = bell_draw(seeds[3], (E_WIN, FF, D), FF ** -0.5, 0.0625, ((0, 4), (1, 8)))
    chosen = draw_chosen(jax.random.fold_in(seeds[7], 71), 0)
    counts = draw_counts(jax.random.fold_in(seeds[7], 71), 0)
    gates = jnp.clip(jnp.exp(math.log(1.0) - 2.9957323 * jax.random.uniform(seeds[6], (IMAGES, E_WIN, CAP), jnp.float32) ** level_of(seeds[6], (IMAGES, E_WIN, CAP), ((0, 32),), -0.2, 0.2)), 0.05, 1.0)
    return dict(tokens_in=tokens_in, out_grad=out_grad, w_in=w_in, w_out=w_out, chosen=chosen, counts=counts, gates=gates)


gelu_coef = 0.7978845608028654


def gelu_parts(hidden):
    inner_arg = gelu_coef * (hidden + 0.044715 * hidden * hidden * hidden)
    tangent = jnp.tanh(inner_arg)
    activation = 0.5 * hidden * (1.0 + tangent)
    slope = 0.5 * (1.0 + tangent) + 0.5 * hidden * (1.0 - tangent * tangent) * gelu_coef * (1.0 + 3.0 * 0.044715 * hidden * hidden)
    return activation, slope


def reference(tokens_in, out_grad, w_in, w_out, chosen, counts, gates):
    image_base = (jnp.arange(IMAGES, dtype=jnp.int32) * LEN)[:, None, None]
    token_rows = (image_base + chosen).astype(jnp.int32)
    slot_iota = jnp.arange(CAP, dtype=jnp.int32)[None, None, :]
    live_gate = jnp.where(slot_iota < counts[:, :, None], gates, jnp.float32(0.0)).astype(jnp.float32)
    rows_by_expert = jnp.transpose(token_rows, (1, 0, 2)).reshape(E_WIN, IMAGES * CAP)
    gate_by_expert = jnp.transpose(live_gate, (1, 0, 2)).reshape(E_WIN, IMAGES * CAP)

    def per_expert(inputs):
        row_ids, gate_col, weight_in, weight_out = inputs
        expert_x = jnp.take(tokens_in, row_ids, axis=0)
        expert_grad = (gate_col[:, None] * jnp.take(out_grad, row_ids, axis=0).astype(jnp.float32)).astype(jnp.bfloat16)
        hidden = jnp.dot(expert_x, weight_in, preferred_element_type=jnp.float32)
        activation, slope = gelu_parts(hidden)
        activation = activation.astype(jnp.bfloat16)
        back_hidden = jnp.dot(expert_grad, weight_out.T, preferred_element_type=jnp.float32)
        hidden_grad = (back_hidden * slope).astype(jnp.bfloat16)
        grad_out_w = jnp.dot(activation.T, expert_grad, preferred_element_type=jnp.float32)
        grad_in_w = jnp.dot(expert_x.T, hidden_grad, preferred_element_type=jnp.float32)
        slot_grad = jnp.dot(hidden_grad, weight_in.T, preferred_element_type=jnp.float32)
        return grad_in_w, grad_out_w, slot_grad

    grad_w_in, grad_w_out, slot_grad = lax.map(per_expert, (rows_by_expert, gate_by_expert, w_in, w_out))
    summed = jnp.zeros((TOKENS, D), jnp.float32).at[rows_by_expert.reshape(-1)].add(slot_grad.reshape(E_WIN * IMAGES * CAP, D))
    return summed.astype(jnp.bfloat16), grad_w_in, grad_w_out
```

```python
import functools

import jax
import jax.numpy as jnp
from jax import lax
from jax.experimental import pallas as pl
from jax.experimental.pallas import tpu as pltpu
from jax.sharding import PartitionSpec as P

gelu_coef = 0.7978845608028654
both = ("group", "fsdp")


def gelu_parts(hidden):
    inner_arg = gelu_coef * (hidden + 0.044715 * hidden * hidden * hidden)
    tangent = jnp.tanh(inner_arg)
    activation = 0.5 * hidden * (1.0 + tangent)
    slope = 0.5 * (1.0 + tangent) + 0.5 * hidden * (1.0 - tangent * tangent) * gelu_coef * (
        1.0 + 3.0 * 0.044715 * hidden * hidden
    )
    return (activation, slope)


def params(limit=48 * 2**20):
    return pltpu.CompilerParams(vmem_limit_bytes=limit)


def cost(flops, moved, trans=0):
    return pl.CostEstimate(flops=flops, bytes_accessed=moved, transcendentals=trans)


def smem():
    return pl.BlockSpec(memory_space=pltpu.SMEM)


def column_of(values, rows, dtype):
    at = lax.broadcasted_iota(jnp.int32, (8, 128), 0)
    tiles = []
    for base in range(0, rows, 8):
        tile = jnp.full((8, 128), values[base], dtype)
        for r in range(1, 8):
            tile = jnp.where(at == r, values[base + r], tile)
        tiles.append(tile)
    return jnp.concatenate(tiles, axis=0)


def pick_kernel(gated, groups, slots, chosen, counts, gates, tokens, *rest):
    outs, onehot, scale = rest[:groups], rest[groups], rest[groups + 1]
    length, width = tokens.shape
    rows = groups * slots

    @pl.when(pl.program_id(0) == 0)
    def _():
        me = lax.axis_index("group")
        owner = [lax.rem(me + r, groups) for r in range(groups)]
        column = column_of([chosen[0, owner[r // slots], r % slots] for r in range(rows)], rows, jnp.int32)
        place = jnp.concatenate([column] * (length // 128), axis=1)
        onehot[...] = jnp.where(
            place == lax.broadcasted_iota(jnp.int32, (rows, length), 1), 1.0, 0.0
        ).astype(jnp.bfloat16)
        if gated:
            live = []
            for r in range(rows):
                e, c = owner[r // slots], r % slots
                live.append(jnp.where(c < counts[0, e], gates[0, e, c], jnp.float32(0.0)))
            scale[...] = column_of(live, rows, jnp.float32)

    picked = jnp.dot(onehot[...], tokens[...], preferred_element_type=jnp.float32)
    if gated:
        picked = picked * jnp.concatenate([scale[...]] * (width // 128), axis=1)
    picked = picked.astype(jnp.bfloat16)
    for d in range(groups):
        outs[d][...] = picked[d * slots : (d + 1) * slots]


def pick(gated, tokens, chosen, counts, gates, groups):
    slots = chosen.shape[2]
    length, model = tokens.shape
    tile = min(512, model)
    rows = groups * slots
    return pl.pallas_call(
        functools.partial(pick_kernel, gated, groups, slots),
        grid=(model // tile,),
        in_specs=[smem(), smem(), smem(), pl.BlockSpec((length, tile), lambda i: (0, i))],
        out_specs=[pl.BlockSpec((slots, tile), lambda i: (0, i))] * groups,
        out_shape=[jax.ShapeDtypeStruct((slots, model), jnp.bfloat16)] * groups,
        scratch_shapes=[pltpu.VMEM((rows, length), jnp.bfloat16), pltpu.VMEM((rows, 128), jnp.float32)],
        compiler_params=params(),
        cost_estimate=cost(2 * rows * length * model, 2 * length * model),
        name="pick_grad" if gated else "pick_x",
    )(chosen, counts, gates, tokens)


def whole_spec(shape):
    return pl.BlockSpec(shape, lambda i: (0,) * len(shape))


def fwd_kernel(x, xp, w, act, slope, lhs):
    half = x.shape[0]

    @pl.when(pl.program_id(0) == 0)
    def _():
        lhs[:half] = x[...]
        lhs[half:] = xp[...]

    hidden = jnp.dot(lhs[...], w[0], preferred_element_type=jnp.float32)
    activation, gelu_slope = gelu_parts(hidden)
    act[...] = activation.astype(jnp.bfloat16)
    slope[...] = gelu_slope


def fwd(x, xp, w_in):
    half, model = x.shape
    units = w_in.shape[2]
    tile = min(256, units)
    rows = 2 * half
    return pl.pallas_call(
        fwd_kernel,
        grid=(units // tile,),
        in_specs=[
            whole_spec((half, model)),
            whole_spec((half, model)),
            pl.BlockSpec((1, model, tile), lambda i: (0, 0, i)),
        ],
        out_specs=[pl.BlockSpec((rows, tile), lambda i: (0, i))] * 2,
        out_shape=[
            jax.ShapeDtypeStruct((rows, units), jnp.bfloat16),
            jax.ShapeDtypeStruct((rows, units), jnp.float32),
        ],
        scratch_shapes=[pltpu.VMEM((rows, model), jnp.bfloat16)],
        compiler_params=params(),
        cost_estimate=cost(2 * rows * model * units, 2 * model * units, rows * units),
        name="hidden",
    )(x, xp, w_in)


def bwd_kernel(g, gp, w_out, w_in, slope, hgrad, mine, theirs, lhs, total):
    half = g.shape[0]
    step = pl.program_id(0)

    @pl.when(step == 0)
    def _():
        lhs[:half] = g[...]
        lhs[half:] = gp[...]

    back = lax.dot_general(
        lhs[...], w_out[0], (((1,), (1,)), ((), ())), preferred_element_type=jnp.float32
    )
    hg = (back * slope[...]).astype(jnp.bfloat16)
    hgrad[...] = hg
    part = lax.dot_general(hg, w_in[0], (((1,), (1,)), ((), ())), preferred_element_type=jnp.float32)

    @pl.when(step == 0)
    def _():
        total[...] = part

    @pl.when(step > 0)
    def _():
        total[...] += part

    @pl.when(step == pl.num_programs(0) - 1)
    def _():
        mine[...] = total[:half]
        theirs[...] = total[half:].astype(theirs.dtype)


def bwd(g, gp, w_out, w_in, slope):
    half, model = g.shape
    units = w_in.shape[2]
    tile = min(256, units)
    rows = 2 * half
    return pl.pallas_call(
        bwd_kernel,
        grid=(units // tile,),
        in_specs=[
            whole_spec((half, model)),
            whole_spec((half, model)),
            pl.BlockSpec((1, tile, model), lambda i: (0, i, 0)),
            pl.BlockSpec((1, model, tile), lambda i: (0, 0, i)),
            pl.BlockSpec((rows, tile), lambda i: (0, i)),
        ],
        out_specs=[
            pl.BlockSpec((rows, tile), lambda i: (0, i)),
            whole_spec((half, model)),
            whole_spec((half, model)),
        ],
        out_shape=[
            jax.ShapeDtypeStruct((rows, units), jnp.bfloat16),
            jax.ShapeDtypeStruct((half, model), jnp.float32),
            jax.ShapeDtypeStruct((half, model), jnp.bfloat16),
        ],
        scratch_shapes=[pltpu.VMEM((rows, model), jnp.bfloat16), pltpu.VMEM((rows, model), jnp.float32)],
        compiler_params=params(),
        cost_estimate=cost(4 * rows * model * units, 4 * model * units),
        name="hidden_grad",
    )(g, gp, w_out, w_in, slope)


def outer_kernel(n_left, *refs):
    left, right, out = refs[:n_left], refs[n_left:-1], refs[-1]
    a = jnp.concatenate([r[...] for r in left], axis=0)
    b = jnp.concatenate([r[...] for r in right], axis=0)
    out[0] = lax.dot_general(a, b, (((0,), (0,)), ((), ())), preferred_element_type=jnp.float32)


def outer(left, right, tile, name):
    m, n = left[0].shape[1], right[0].shape[1]
    rows = sum(r.shape[0] for r in left)
    tile = min(tile, m)
    return pl.pallas_call(
        functools.partial(outer_kernel, len(left)),
        grid=(m // tile,),
        in_specs=[pl.BlockSpec((r.shape[0], tile), lambda i: (0, i)) for r in left]
        + [whole_spec(r.shape) for r in right],
        out_specs=pl.BlockSpec((1, tile, n), lambda i: (0, i, 0)),
        out_shape=jax.ShapeDtypeStruct((1, m, n), jnp.float32),
        compiler_params=params(),
        cost_estimate=cost(2 * rows * m * n, 4 * m * n),
        name=name,
    )(*left, *right)


def add_kernel(n_in, *refs):
    ins, outs = refs[:n_in], refs[n_in:]
    total = ins[0][...].astype(jnp.float32)
    for r in ins[1:]:
        total = total + r[...].astype(jnp.float32)
    total = total.astype(jnp.bfloat16)
    rows = outs[0].shape[0]
    for i, out in enumerate(outs):
        out[...] = total[i * rows : (i + 1) * rows]


def add_up(ins, pieces):
    rows, model = ins[0].shape
    return pl.pallas_call(
        functools.partial(add_kernel, len(ins)),
        out_shape=[jax.ShapeDtypeStruct((rows // pieces, model), jnp.bfloat16)] * pieces,
        compiler_params=params(),
        cost_estimate=cost(rows * model, 12 * rows * model),
        name="add_up",
    )(*ins)


def place_kernel(groups, slots, chosen, *rest):
    parts, out, onehot = rest[:-2], rest[-2], rest[-1]
    length, width = out.shape
    rows = len(parts) * slots

    @pl.when(pl.program_id(0) == 0)
    def _():
        me = lax.axis_index("group")
        lane = lax.broadcasted_iota(jnp.int32, (8, rows), 1)
        place = jnp.full((8, rows), -1, jnp.int32)
        for d in range(groups):
            owner = lax.rem(me + d, groups)
            for c in range(slots):
                hit = lane == d * slots + c
                for again in range(1, len(parts) // groups):
                    hit = hit | (lane == (again * groups + d) * slots + c)
                place = jnp.where(hit, chosen[0, owner, c], place)
        place = jnp.concatenate([place] * (length // 8), axis=0)
        onehot[...] = jnp.where(
            place == lax.broadcasted_iota(jnp.int32, (length, rows), 0), 1.0, 0.0
        ).astype(jnp.bfloat16)

    values = jnp.concatenate([p[...] for p in parts], axis=0)
    out[...] = jnp.dot(onehot[...], values, preferred_element_type=jnp.float32).astype(jnp.bfloat16)


def place(parts, chosen, length, groups):
    slots = chosen.shape[2]
    model = parts[0].shape[1]
    tile = min(512, model)
    rows = len(parts) * slots
    return pl.pallas_call(
        functools.partial(place_kernel, groups, slots),
        grid=(model // tile,),
        in_specs=[smem()] + [pl.BlockSpec((slots, tile), lambda i: (0, i))] * len(parts),
        out_specs=pl.BlockSpec((length, tile), lambda i: (0, i)),
        out_shape=jax.ShapeDtypeStruct((length, model), jnp.bfloat16),
        scratch_shapes=[pltpu.VMEM((length, rows), jnp.bfloat16)],
        compiler_params=params(),
        cost_estimate=cost(2 * rows * length * model, 2 * length * model),
        name="place",
    )(chosen, *parts)


def shards(tokens_in, out_grad, w_in, w_out, chosen, counts, gates):
    groups = lax.axis_size("group")
    fsdp = lax.axis_size("fsdp")
    ring_len = fsdp // 2

    def send(x, group_step, chip_step):
        pairs = [
            (g * fsdp + f, (g + group_step) % groups * fsdp + (f + 2 * chip_step) % fsdp)
            for g in range(groups)
            for f in range(fsdp)
        ]
        return lax.ppermute(x, both, pairs)

    def ring(x):
        return lax.ppermute(x, "fsdp", [(f, (f + 2) % fsdp) for f in range(fsdp)])

    def pair(x):
        return lax.ppermute(x, "fsdp", [(f, f ^ 1) for f in range(fsdp)])

    def spread(pieces):
        next_pieces = [send(pieces[d], d, 1) for d in range(groups)]
        own_pieces = [pieces[0]] + [send(pieces[d], d, 0) for d in range(1, groups)]
        blocks = [jnp.concatenate(own_pieces, axis=0), jnp.concatenate(next_pieces, axis=0)]
        while len(blocks) < ring_len:
            blocks.append(ring(blocks[-1]))
        return blocks

    picked_x = pick(False, tokens_in, chosen, counts, gates, groups)
    picked_grad = pick(True, out_grad, chosen, counts, gates, groups)
    xs = spread(picked_x)
    gs = spread(picked_grad)
    xps = [pair(x) for x in xs]
    gps = [pair(g) for g in gs]

    acts, hgrads, mines, pair_parts = [], [], [], []
    for k in range(ring_len):
        act, slope = fwd(xs[k], xps[k], w_in)
        hgrad, mine, theirs = bwd(gs[k], gps[k], w_out, w_in, slope)
        acts.append(act)
        hgrads.append(hgrad)
        mines.append(mine)
        pair_parts.append(pair(theirs))

    own = add_up([mines[0], pair_parts[0]], groups)
    running = []
    for k in range(1, ring_len):
        last = k == ring_len - 1
        pieces = add_up([mines[k], pair_parts[k]] + running, groups if last else 1)
        if not last:
            running = [ring(pieces[0])]
    parts = [own[0]] + [send(own[d], -d, 0) for d in range(1, groups)]
    parts += [send(pieces[d], -d, 1) for d in range(groups)]

    grad_w_in = outer([r for k in range(ring_len) for r in (xs[k], xps[k])], hgrads, 512, "grad_w_in")
    grad_w_out = outer(acts, [r for k in range(ring_len) for r in (gs[k], gps[k])], 256, "grad_w_out")
    return place(parts, chosen, tokens_in.shape[0], groups), grad_w_in, grad_w_out


def solution(mesh):
    placed = (
        P(("group", "fsdp"), None),
        P(("group", "fsdp"), None),
        P("group", None, "fsdp"),
        P("group", "fsdp", None),
        P(("group", "fsdp"), None, None),
        P(("group", "fsdp"), None),
        P(("group", "fsdp"), None, None),
    )
    return jax.shard_map(
        shards,
        mesh=mesh,
        in_specs=placed,
        out_specs=(P(("group", "fsdp"), None), P("group", None, "fsdp"), P("group", "fsdp", None)),
        check_vma=False,
    )
```

```python
import functools

import jax
import jax.numpy as jnp
from jax import lax
from jax.experimental import pallas as pl
from jax.experimental.pallas import tpu as pltpu
from jax.sharding import PartitionSpec as P

gelu_coef = 0.7978845608028654
both = ("group", "fsdp")


def gelu_parts(hidden):
    inner_arg = gelu_coef * (hidden + 0.044715 * hidden * hidden * hidden)
    tangent = jnp.tanh(inner_arg)
    activation = 0.5 * hidden * (1.0 + tangent)
    slope = 0.5 * (1.0 + tangent) + 0.5 * hidden * (1.0 - tangent * tangent) * gelu_coef * (
        1.0 + 3.0 * 0.044715 * hidden * hidden
    )
    return (activation, slope)


def params(limit=48 * 2**20):
    return pltpu.CompilerParams(vmem_limit_bytes=limit)


def cost(flops, moved, trans=0):
    return pl.CostEstimate(flops=flops, bytes_accessed=moved, transcendentals=trans)


def smem():
    return pl.BlockSpec(memory_space=pltpu.SMEM)


def column_of(values, rows, dtype):
    at = lax.broadcasted_iota(jnp.int32, (8, 128), 0)
    tiles = []
    for base in range(0, rows, 8):
        tile = jnp.full((8, 128), values[base], dtype)
        for r in range(1, 8):
            tile = jnp.where(at == r, values[base + r], tile)
        tiles.append(tile)
    return jnp.concatenate(tiles, axis=0)


def pick_kernel(groups, slots, chosen, counts, gates, tokens, grads, *rest):
    outs, spot, onehot, scale = rest[:groups], rest[groups], rest[groups + 1], rest[groups + 2]
    length, width = tokens.shape
    rows = groups * slots

    @pl.when(pl.program_id(0) == 0)
    def _():
        me = lax.axis_index("group")
        owner = [lax.rem(me + r, groups) for r in range(groups)]
        where = [chosen[0, owner[r // slots], r % slots] for r in range(rows)]
        column = jnp.concatenate([column_of(where, rows, jnp.int32)] * (length // 128), axis=1)
        onehot[...] = jnp.where(
            column == lax.broadcasted_iota(jnp.int32, (rows, length), 1), 1.0, 0.0
        ).astype(jnp.bfloat16)
        live = []
        for r in range(rows):
            e, c = owner[r // slots], r % slots
            live.append(jnp.where(c < counts[0, e], gates[0, e, c], jnp.float32(0.0)))
        scale[...] = column_of(live, rows, jnp.float32)
        lane = lax.rem(lax.broadcasted_iota(jnp.int32, (8, 2 * rows), 1), rows)
        line = jnp.full((8, 2 * rows), -1, jnp.int32)
        for r in range(rows):
            line = jnp.where(lane == r, where[r], line)
        line = jnp.concatenate([line] * (length // 8), axis=0)
        spot[...] = jnp.where(
            line == lax.broadcasted_iota(jnp.int32, (length, 2 * rows), 0), 1.0, 0.0
        ).astype(jnp.bfloat16)

    x = jnp.dot(onehot[...], tokens[...], preferred_element_type=jnp.float32).astype(jnp.bfloat16)
    g = jnp.dot(onehot[...], grads[...], preferred_element_type=jnp.float32)
    g = (g * jnp.concatenate([scale[...]] * (width // 128), axis=1)).astype(jnp.bfloat16)
    for d in range(groups):
        outs[d][:slots] = x[d * slots : (d + 1) * slots]
        outs[d][slots:] = g[d * slots : (d + 1) * slots]


def pick(tokens, grads, chosen, counts, gates, groups):
    slots = chosen.shape[2]
    length, model = tokens.shape
    tile = min(512, model)
    rows = groups * slots
    return pl.pallas_call(
        functools.partial(pick_kernel, groups, slots),
        grid=(model // tile,),
        in_specs=[smem(), smem(), smem()] + [pl.BlockSpec((length, tile), lambda i: (0, i))] * 2,
        out_specs=[pl.BlockSpec((2 * slots, tile), lambda i: (0, i))] * groups
        + [whole_spec((length, 2 * rows))],
        out_shape=[jax.ShapeDtypeStruct((2 * slots, model), jnp.bfloat16)] * groups
        + [jax.ShapeDtypeStruct((length, 2 * rows), jnp.bfloat16)],
        scratch_shapes=[pltpu.VMEM((rows, length), jnp.bfloat16), pltpu.VMEM((rows, 128), jnp.float32)],
        compiler_params=params(60 * 2**20),
        cost_estimate=cost(4 * rows * length * model, 4 * length * model),
        name="pick",
    )(chosen, counts, gates, tokens, grads)


def whole_spec(shape):
    return pl.BlockSpec(shape, lambda i: (0,) * len(shape))


def block_kernel(slots, n_in, *refs):
    ins = refs[:n_in]
    w_in, w_out, x_t, act_t, hgrad, g_all, mine, theirs, x_all, g_t, total = refs[n_in:]
    step = pl.program_id(0)
    half = mine.shape[0]

    @pl.when(step == 0)
    def _():
        at = 0
        for ref in ins:
            for row in range(0, ref.shape[0], 2 * slots):
                x_all[at : at + slots] = ref[row : row + slots]
                g_all[at : at + slots] = ref[row + slots : row + 2 * slots]
                at += slots
        x_t[...] = x_all[...].T
        g_t[...] = g_all[...].T

    hidden = jnp.dot(x_all[...], w_in[0], preferred_element_type=jnp.float32).T
    activation, gelu_slope = gelu_parts(hidden)
    act_t[...] = activation.astype(jnp.bfloat16)
    back = jnp.dot(w_out[0], g_t[...], preferred_element_type=jnp.float32)
    hg_t = (back * gelu_slope).astype(jnp.bfloat16)
    hgrad[...] = hg_t.T
    part = jnp.dot(w_in[0], hg_t, preferred_element_type=jnp.float32)

    @pl.when(step == 0)
    def _():
        total[...] = part

    @pl.when(step > 0)
    def _():
        total[...] += part

    @pl.when(step == pl.num_programs(0) - 1)
    def _():
        slot_grad = total[...].T
        mine[...] = slot_grad[:half]
        theirs[...] = slot_grad[half:].astype(theirs.dtype)


def block(ins, w_in, w_out, slots):
    model = w_in.shape[1]
    units = w_in.shape[2]
    rows = sum(r.shape[0] for r in ins) // 2
    half = rows // 2
    tile = min(256, units)
    bf = functools.partial(jax.ShapeDtypeStruct, dtype=jnp.bfloat16)
    return pl.pallas_call(
        functools.partial(block_kernel, slots, len(ins)),
        grid=(units // tile,),
        in_specs=[whole_spec(r.shape) for r in ins]
        + [
            pl.BlockSpec((1, model, tile), lambda i: (0, 0, i)),
            pl.BlockSpec((1, tile, model), lambda i: (0, i, 0)),
        ],
        out_specs=[
            whole_spec((model, rows)),
            pl.BlockSpec((tile, rows), lambda i: (i, 0)),
            pl.BlockSpec((rows, tile), lambda i: (0, i)),
            whole_spec((rows, model)),
            whole_spec((half, model)),
            whole_spec((half, model)),
        ],
        out_shape=[
            bf((model, rows)),
            bf((units, rows)),
            bf((rows, units)),
            bf((rows, model)),
            jax.ShapeDtypeStruct((half, model), jnp.float32),
            bf((half, model)),
        ],
        scratch_shapes=[
            pltpu.VMEM((rows, model), jnp.bfloat16),
            pltpu.VMEM((model, rows), jnp.bfloat16),
            pltpu.VMEM((model, rows), jnp.float32),
        ],
        compiler_params=params(),
        cost_estimate=cost(6 * rows * model * units, 4 * model * units, rows * units),
        name="block",
    )(*ins, w_in, w_out)


def outer_kernel(n, *refs):
    left, right, out = refs[:n], refs[n:-1], refs[-1]
    a = jnp.concatenate([r[...] for r in left], axis=1)
    b = jnp.concatenate([r[...] for r in right], axis=0)
    out[0] = jnp.dot(a, b, preferred_element_type=jnp.float32)


def outer(left_t, right, tile, name):
    m, n = left_t[0].shape[0], right[0].shape[1]
    rows = sum(r.shape[0] for r in right)
    tile = min(tile, m)
    return pl.pallas_call(
        functools.partial(outer_kernel, len(right)),
        grid=(m // tile,),
        in_specs=[pl.BlockSpec((tile, r.shape[1]), lambda i: (i, 0)) for r in left_t]
        + [whole_spec(r.shape) for r in right],
        out_specs=pl.BlockSpec((1, tile, n), lambda i: (0, i, 0)),
        out_shape=jax.ShapeDtypeStruct((1, m, n), jnp.float32),
        compiler_params=params(),
        cost_estimate=cost(2 * rows * m * n, 4 * m * n),
        name=name,
    )(*left_t, *right)


def add_kernel(plan, n_in, *refs):
    ins, outs = refs[:n_in], refs[n_in:]
    total = ins[0][...].astype(jnp.float32)
    for r in ins[1:]:
        if r.shape == total.shape:
            total = total + r[...].astype(jnp.float32)
    total = total.astype(jnp.bfloat16)
    at = 0
    for out in outs:
        out[...] = total[at : at + out.shape[0]]
        at += out.shape[0]


def add_up(ins, cuts):
    rows, model = ins[0].shape
    return pl.pallas_call(
        functools.partial(add_kernel, None, len(ins)),
        out_shape=[jax.ShapeDtypeStruct((c, model), jnp.bfloat16) for c in cuts],
        compiler_params=params(),
        cost_estimate=cost(rows * model, 12 * rows * model),
        name="add_up",
    )(*ins)


def place_kernel(spot, *rest):
    parts, out = rest[:-1], rest[-1]
    values = jnp.concatenate([p[...] for p in parts], axis=0)
    out[...] = jnp.dot(spot[...], values, preferred_element_type=jnp.float32).astype(jnp.bfloat16)


def place(parts, spot):
    slots, model = parts[0].shape
    length, rows = spot.shape
    tile = min(512, model)
    return pl.pallas_call(
        place_kernel,
        grid=(model // tile,),
        in_specs=[whole_spec(spot.shape)] + [pl.BlockSpec((slots, tile), lambda i: (0, i))] * len(parts),
        out_specs=pl.BlockSpec((length, tile), lambda i: (0, i)),
        out_shape=jax.ShapeDtypeStruct((length, model), jnp.bfloat16),
        compiler_params=params(),
        cost_estimate=cost(2 * rows * length * model, 2 * length * model),
        name="place",
    )(spot, *parts)


def shards(tokens_in, out_grad, w_in, w_out, chosen, counts, gates):
    groups = lax.axis_size("group")
    fsdp = lax.axis_size("fsdp")
    ring_len = fsdp // 2
    slots = chosen.shape[2]
    rows = groups * slots

    def send(x, group_step, chip_step):
        pairs = [
            (g * fsdp + f, (g + group_step) % groups * fsdp + (f + 2 * chip_step) % fsdp)
            for g in range(groups)
            for f in range(fsdp)
        ]
        return lax.ppermute(x, both, pairs)

    def ring(x):
        return lax.ppermute(x, "fsdp", [(f, (f + 2) % fsdp) for f in range(fsdp)])

    def pair(x):
        return lax.ppermute(x, "fsdp", [(f, f ^ 1) for f in range(fsdp)])

    *picked, spot = pick(tokens_in, out_grad, chosen, counts, gates, groups)
    cut = groups // 2
    ahead = [send(picked[d], d, 1) for d in range(groups)]
    near = [picked[0]] + [send(picked[d], d, 0) for d in range(1, groups)]
    chains = [[jnp.concatenate(near, axis=0)]]
    chains.append([jnp.concatenate(ahead[:cut], axis=0), jnp.concatenate(ahead[cut:], axis=0)])
    while len(chains) < ring_len:
        chains.append([ring(x) for x in chains[-1]])
    paired = [[pair(x) for x in chain] for chain in chains]

    results = [block(chains[0] + chains[1] + paired[0] + paired[1], w_in, w_out, slots)]
    for k in range(2, ring_len):
        results.append(block(chains[k] + paired[k], w_in, w_out, slots))
    x_ts, act_ts, hgrads, gs, mines, theirs = zip(*results)

    parts, running = [], []
    for i, (mine, other) in enumerate(zip(mines, theirs)):
        last = i == len(mines) - 1
        cuts = [slots] * groups if i == 0 else []
        cuts = cuts + ([slots] * groups if last else [rows])
        pieces = add_up([mine, pair(other)] + running, cuts)
        if i == 0:
            parts += [pieces[0]] + [send(pieces[d], -d, 0) for d in range(1, groups)]
            pieces = pieces[groups:]
        if not last:
            running = [ring(pieces[0])]
    parts += [send(pieces[d], -d, 1) for d in range(groups)]

    grad_w_in = outer(x_ts, hgrads, 512, "grad_w_in")
    grad_w_out = outer(act_ts, gs, 256, "grad_w_out")
    return place(parts, spot), grad_w_in, grad_w_out


def solution(mesh):
    placed = (
        P(("group", "fsdp"), None),
        P(("group", "fsdp"), None),
        P("group", None, "fsdp"),
        P("group", "fsdp", None),
        P(("group", "fsdp"), None, None),
        P(("group", "fsdp"), None),
        P(("group", "fsdp"), None, None),
    )
    return jax.shard_map(
        shards,
        mesh=mesh,
        in_specs=placed,
        out_specs=(P(("group", "fsdp"), None), P("group", None, "fsdp"), P("group", "fsdp", None)),
        check_vma=False,
    )
```

```python
import functools

import jax
import jax.numpy as jnp
from jax import lax
from jax.experimental import pallas as pl
from jax.experimental.pallas import tpu as pltpu
from jax.sharding import PartitionSpec as P

gelu_coef = 0.7978845608028654
both = ("group", "fsdp")


def gelu_parts(hidden):
    inner_arg = gelu_coef * (hidden + 0.044715 * hidden * hidden * hidden)
    tangent = jnp.tanh(inner_arg)
    activation = 0.5 * hidden * (1.0 + tangent)
    slope = 0.5 * (1.0 + tangent) + 0.5 * hidden * (1.0 - tangent * tangent) * gelu_coef * (
        1.0 + 3.0 * 0.044715 * hidden * hidden
    )
    return (activation, slope)


def params(limit=48 * 2**20):
    return pltpu.CompilerParams(vmem_limit_bytes=limit)


def cost(flops, moved, trans=0):
    return pl.CostEstimate(flops=flops, bytes_accessed=moved, transcendentals=trans)


def column_of(values, rows, dtype):
    at = lax.broadcasted_iota(jnp.int32, (8, 128), 0)
    tiles = []
    for base in range(0, rows, 8):
        tile = jnp.full((8, 128), values[base], dtype)
        for r in range(1, 8):
            tile = jnp.where(at == r, values[base + r], tile)
        tiles.append(tile)
    return jnp.concatenate(tiles, axis=0)


def pick_kernel(groups, slots, tiles, chosen_in, counts_in, gates_in, tokens_in, grads_in, *rest):
    outs, spot = rest[: 2 * groups], rest[2 * groups]
    chosen, counts, gates, tokens, grads, small, big = rest[2 * groups + 1 :]
    length, model = tokens.shape
    rows = groups * slots
    width = model // tiles
    scalars = [
        pltpu.make_async_copy(src, dst, small.at[i])
        for i, (src, dst) in enumerate(((chosen_in, chosen), (counts_in, counts), (gates_in, gates)))
    ]
    loads = []
    for i in range(tiles):
        some = slice(i * width, (i + 1) * width)
        for j, (src, dst) in enumerate(((tokens_in, tokens), (grads_in, grads))):
            loads.append(pltpu.make_async_copy(src.at[:, some], dst.at[:, some], big.at[2 * i + j]))
    for copy in scalars + loads:
        copy.start()
    for copy in scalars:
        copy.wait()

    me = lax.axis_index("group")
    owner = [lax.bitwise_xor(me, r) for r in range(groups)]
    where = [chosen[0, owner[r // slots], r % slots] for r in range(rows)]
    column = jnp.concatenate([column_of(where, rows, jnp.int32)] * (length // 128), axis=1)
    onehot = jnp.where(column == lax.broadcasted_iota(jnp.int32, (rows, length), 1), 1.0, 0.0).astype(
        jnp.bfloat16
    )
    live = []
    for r in range(rows):
        e, c = owner[r // slots], r % slots
        live.append(jnp.where(c < counts[0, e], gates[0, e, c], jnp.float32(0.0)))
    scale = jnp.concatenate([column_of(live, rows, jnp.float32)] * (width // 128), axis=1)
    lane = lax.rem(lax.broadcasted_iota(jnp.int32, (8, 2 * rows), 1), rows)
    line = jnp.full((8, 2 * rows), -1, jnp.int32)
    for r in range(rows):
        line = jnp.where(lane == r, where[r], line)
    line = jnp.concatenate([line] * (length // 8), axis=0)
    spot[...] = jnp.where(
        line == lax.broadcasted_iota(jnp.int32, (length, 2 * rows), 0), 1.0, 0.0
    ).astype(jnp.bfloat16)

    for i in range(tiles):
        some = slice(i * width, (i + 1) * width)
        loads[2 * i].wait()
        x = jnp.dot(onehot, tokens[:, some], preferred_element_type=jnp.float32).astype(jnp.bfloat16)
        loads[2 * i + 1].wait()
        g = jnp.dot(onehot, grads[:, some], preferred_element_type=jnp.float32)
        g = (g * scale).astype(jnp.bfloat16)
        for j, out in enumerate(outs):
            d = j % groups
            out[:slots, some] = x[d * slots : (d + 1) * slots]
            out[slots:, some] = g[d * slots : (d + 1) * slots]


def pick(tokens, grads, chosen, counts, gates, groups):
    slots = chosen.shape[2]
    length, model = tokens.shape
    tiles = max(1, model // 512)
    rows = groups * slots
    return pl.pallas_call(
        functools.partial(pick_kernel, groups, slots, tiles),
        in_specs=[anywhere()] * 5,
        out_specs=[vmem()] * (2 * groups + 1),
        out_shape=[jax.ShapeDtypeStruct((2 * slots, model), jnp.bfloat16)] * (2 * groups)
        + [jax.ShapeDtypeStruct((length, 2 * rows), jnp.bfloat16)],
        scratch_shapes=[
            pltpu.SMEM(chosen.shape, chosen.dtype),
            pltpu.SMEM(counts.shape, counts.dtype),
            pltpu.SMEM(gates.shape, gates.dtype),
            pltpu.VMEM((length, model), jnp.bfloat16),
            pltpu.VMEM((length, model), jnp.bfloat16),
            pltpu.SemaphoreType.DMA((3,)),
            pltpu.SemaphoreType.DMA((2 * tiles,)),
        ],
        compiler_params=params(60 * 2**20),
        cost_estimate=cost(4 * rows * length * model, 4 * length * model),
        name="pick",
    )(chosen, counts, gates, tokens, grads)


def vmem():
    return pl.BlockSpec(memory_space=pltpu.VMEM)


def anywhere():
    return pl.BlockSpec(memory_space=pl.ANY)


def join_kernel(n, *refs):
    out = refs[-1]
    at = 0
    for ref in refs[:n]:
        out[at : at + ref.shape[0]] = ref[...]
        at += ref.shape[0]


def join(ins, after):
    rows, model = sum(r.shape[0] for r in ins), ins[0].shape[1]
    return pl.pallas_call(
        functools.partial(join_kernel, len(ins)),
        in_specs=[vmem()] * len(ins) + [anywhere()] * len(after),
        out_specs=vmem(),
        out_shape=jax.ShapeDtypeStruct((rows, model), jnp.bfloat16),
        compiler_params=params(10 * 2**20),
        cost_estimate=cost(0, 4 * rows * model),
        name="join",
    )(*ins, *after)


def block_kernel(slots, tile, n_in, *refs):
    ins, (w_in, w_out) = refs[:n_in], refs[n_in : n_in + 2]
    x_t, act_t, hgrad, g_all, mine, theirs, x_all, g_t, total = refs[-9:]
    half = mine.shape[0]
    at = 0
    for ref in ins:
        for row in range(0, ref.shape[0], 2 * slots):
            x_all[at : at + slots] = ref[row : row + slots]
            g_all[at : at + slots] = ref[row + slots : row + 2 * slots]
            at += slots
    x_t[...] = x_all[...].T
    g_t[...] = g_all[...].T
    for unit in range(0, w_in.shape[2], tile):
        some = slice(unit, unit + tile)
        hidden = jnp.dot(x_all[...], w_in[0, :, some], preferred_element_type=jnp.float32).T
        activation, gelu_slope = gelu_parts(hidden)
        act_t[some] = activation.astype(jnp.bfloat16)
        back = jnp.dot(w_out[0, some], g_t[...], preferred_element_type=jnp.float32)
        hg_t = (back * gelu_slope).astype(jnp.bfloat16)
        hgrad[:, some] = hg_t.T
        part = jnp.dot(w_in[0, :, some], hg_t, preferred_element_type=jnp.float32)
        if unit == 0:
            total[...] = part
        else:
            total[...] += part
    slot_grad = total[...].T
    mine[...] = slot_grad[:half]
    theirs[...] = slot_grad[half:].astype(theirs.dtype)


def block(ins, w_in, w_out, slots, after):
    model, units = w_in.shape[1:]
    rows = sum(r.shape[0] for r in ins) // 2
    half = rows // 2
    bf = functools.partial(jax.ShapeDtypeStruct, dtype=jnp.bfloat16)
    return pl.pallas_call(
        functools.partial(block_kernel, slots, min(256, units), len(ins)),
        in_specs=[vmem()] * (len(ins) + 2) + [anywhere()] * len(after),
        out_specs=[vmem()] * 6,
        out_shape=[
            bf((model, rows)),
            bf((units, rows)),
            bf((rows, units)),
            bf((rows, model)),
            jax.ShapeDtypeStruct((half, model), jnp.float32),
            bf((half, model)),
        ],
        scratch_shapes=[
            pltpu.VMEM((rows, model), jnp.bfloat16),
            pltpu.VMEM((model, rows), jnp.bfloat16),
            pltpu.VMEM((model, rows), jnp.float32),
        ],
        compiler_params=params(20 * 2**20),
        cost_estimate=cost(6 * rows * model * units, 4 * model * units, rows * units),
        name="block",
    )(*ins, w_in, w_out, *after)


def outer_kernel(n, tiles, *refs):
    left_t, right = refs[:n], refs[n : 2 * n]
    out, buf, sems = refs[-3:]
    b = jnp.concatenate([r[...] for r in right], axis=0)
    size = buf.shape[0] // tiles
    copies = []
    for i in range(tiles):
        some = slice(i * size, (i + 1) * size)
        a = jnp.concatenate([r[some] for r in left_t], axis=1)
        buf[some] = jnp.dot(a, b, preferred_element_type=jnp.float32)
        copies.append(pltpu.make_async_copy(buf.at[some], out.at[0, some], sems.at[i]))
        copies[-1].start()
    for copy in copies:
        copy.wait()


def outer(left_ts, rights, after, name):
    n, m, k = len(rights), left_ts[0].shape[0], rights[0].shape[1]
    rows = sum(r.shape[0] for r in rights)
    tiles = 4
    return pl.pallas_call(
        functools.partial(outer_kernel, n, tiles),
        in_specs=[vmem()] * (2 * n) + [anywhere()] * len(after),
        out_specs=anywhere(),
        out_shape=jax.ShapeDtypeStruct((1, m, k), jnp.float32),
        scratch_shapes=[pltpu.VMEM((m, k), jnp.float32), pltpu.SemaphoreType.DMA((tiles,))],
        compiler_params=params(20 * 2**20),
        cost_estimate=cost(2 * rows * m * k, 4 * m * k),
        name=name,
    )(*left_ts, *rights, *after)


def add_kernel(n_in, *refs):
    ins, outs = refs[:n_in], refs[n_in:]
    total = ins[0][...].astype(jnp.float32)
    for ref in ins[1:]:
        total = total + ref[...].astype(jnp.float32)
    total = total.astype(jnp.bfloat16)
    at = 0
    for out in outs:
        out[...] = total[at : at + out.shape[0]]
        at += out.shape[0]


def add_up(ins, cuts):
    rows, model = sum(cuts), ins[0].shape[1]
    return pl.pallas_call(
        functools.partial(add_kernel, len(ins)),
        in_specs=[vmem()] * len(ins),
        out_specs=[vmem()] * len(cuts),
        out_shape=[jax.ShapeDtypeStruct((c, model), jnp.bfloat16) for c in cuts],
        compiler_params=params(10 * 2**20),
        cost_estimate=cost(rows * model, 12 * rows * model),
        name="add_up",
    )(*ins)


def place_kernel(tiles, spot, *rest):
    parts, (out, buf, sems) = rest[:-3], rest[-3:]
    values = jnp.concatenate([p[...] for p in parts], axis=0)
    size = buf.shape[0] // tiles
    copies = []
    for i in range(tiles):
        some = slice(i * size, (i + 1) * size)
        buf[some] = jnp.dot(spot[some], values, preferred_element_type=jnp.float32).astype(jnp.bfloat16)
        copies.append(pltpu.make_async_copy(buf.at[some], out.at[some], sems.at[i]))
        copies[-1].start()
    for copy in copies:
        copy.wait()


def place(parts, spot):
    model = parts[0].shape[1]
    length, rows = spot.shape
    tiles = 4
    return pl.pallas_call(
        functools.partial(place_kernel, tiles),
        in_specs=[vmem()] * (1 + len(parts)),
        out_specs=anywhere(),
        out_shape=jax.ShapeDtypeStruct((length, model), jnp.bfloat16),
        scratch_shapes=[pltpu.VMEM((length, model), jnp.bfloat16), pltpu.SemaphoreType.DMA((tiles,))],
        compiler_params=params(10 * 2**20),
        cost_estimate=cost(2 * rows * length * model, 2 * length * model),
        name="place",
    )(spot, *parts)


def shards(tokens_in, out_grad, w_in, w_out, chosen, counts, gates):
    groups = lax.axis_size("group")
    fsdp = lax.axis_size("fsdp")
    ring_len = fsdp // 2
    slots = chosen.shape[2]

    def send(x, group_step, to):
        pairs = [
            (g * fsdp + f, (g ^ group_step) * fsdp + to(f)) for g in range(groups) for f in range(fsdp)
        ]
        return lax.ppermute(x, both, pairs)

    def ring(x):
        return lax.ppermute(x, "fsdp", [(f, (f + 2) % fsdp) for f in range(fsdp)])

    def pair(x):
        return lax.ppermute(x, "fsdp", [(f, f ^ 1) for f in range(fsdp)])

    *picked, spot = pick(tokens_in, out_grad, chosen, counts, gates, groups)
    order = range(groups - 1, -1, -1)
    near = {d: send(picked[d], d, lambda f: f) if d else picked[d] for d in order}
    next_ = {d: send(picked[groups + d], d, lambda f: (f + 2) % fsdp) for d in order}
    rows = groups * slots
    first = join([near[d] for d in range(groups)], [])
    ours = join([next_[d] for d in range(groups)], [first])
    results, arrived, before = [], [], []
    for k in range(1, ring_len):
        last = k == ring_len - 1
        ahead = None if last else ring(ours)
        mixed = [first, ours, pair(first), pair(ours)] if k == 1 else [ours, pair(ours)]
        results.append(block(mixed, w_in, w_out, slots, before))
        mine, theirs = results[-1][4:]
        cuts = [slots] * groups if last else [rows]
        pieces = add_up([mine, pair(theirs)] + arrived, [slots] * groups + cuts if k == 1 else cuts)
        if k == 1:
            own = [pieces[0]] + [send(pieces[d], d, lambda f: f) for d in range(1, groups)]
            pieces = pieces[groups:]
        before, after = pieces[:1], [theirs] + arrived
        if not last:
            arrived = [ring(pieces[0])]
            ours = join([ahead], after + (own[1:] if k == 2 else []))
    parts = own + [send(pieces[d], d, lambda f: (f + 2) % fsdp) for d in range(groups)]

    x_ts, act_ts, hgrads, gs = list(zip(*results))[:4]
    grad_w_out = outer(act_ts, gs, [], "grad_w_out")
    grad_w_in = outer(x_ts, hgrads, pieces[:1], "grad_w_in")
    return place(parts, spot), grad_w_in, grad_w_out


def solution(mesh):
    placed = (
        P(("group", "fsdp"), None),
        P(("group", "fsdp"), None),
        P("group", None, "fsdp"),
        P("group", "fsdp", None),
        P(("group", "fsdp"), None, None),
        P(("group", "fsdp"), None),
        P(("group", "fsdp"), None, None),
    )
    return jax.shard_map(
        shards,
        mesh=mesh,
        in_specs=placed,
        out_specs=(P(("group", "fsdp"), None), P("group", None, "fsdp"), P("group", "fsdp", None)),
        check_vma=False,
    )
```

```python
import functools

import jax
import jax.numpy as jnp
from jax import lax
from jax.experimental import pallas as pl
from jax.experimental.pallas import tpu as pltpu
from jax.sharding import PartitionSpec as P

gelu_coef = 0.7978845608028654
both = ("group", "fsdp")


def gelu_parts(hidden):
    inner_arg = gelu_coef * (hidden + 0.044715 * hidden * hidden * hidden)
    tangent = jnp.tanh(inner_arg)
    activation = 0.5 * hidden * (1.0 + tangent)
    slope = 0.5 * (1.0 + tangent) + 0.5 * hidden * (1.0 - tangent * tangent) * gelu_coef * (
        1.0 + 3.0 * 0.044715 * hidden * hidden
    )
    return (activation, slope)


def params(limit=48 * 2**20):
    return pltpu.CompilerParams(vmem_limit_bytes=limit)


def cost(flops, moved, trans=0):
    return pl.CostEstimate(flops=flops, bytes_accessed=moved, transcendentals=trans)


def column_of(values, rows, dtype):
    at = lax.broadcasted_iota(jnp.int32, (8, 128), 0)
    tiles = []
    for base in range(0, rows, 8):
        tile = jnp.full((8, 128), values[base], dtype)
        for r in range(1, 8):
            tile = jnp.where(at == r, values[base + r], tile)
        tiles.append(tile)
    return jnp.concatenate(tiles, axis=0)


def pick_kernel(groups, slots, tiles, chosen_in, counts_in, gates_in, tokens_in, grads_in, *rest):
    outs, spot = rest[: 2 * groups], rest[2 * groups]
    chosen, counts, gates, tokens, grads, small, big = rest[2 * groups + 1 :]
    length, model = tokens.shape
    rows = groups * slots
    width = model // tiles
    scalars = [
        pltpu.make_async_copy(src, dst, small.at[i])
        for i, (src, dst) in enumerate(((chosen_in, chosen), (counts_in, counts), (gates_in, gates)))
    ]
    loads = []
    for i in range(tiles):
        some = slice(i * width, (i + 1) * width)
        for j, (src, dst) in enumerate(((tokens_in, tokens), (grads_in, grads))):
            loads.append(pltpu.make_async_copy(src.at[:, some], dst.at[:, some], big.at[2 * i + j]))
    for copy in scalars + loads:
        copy.start()
    for copy in scalars:
        copy.wait()

    me = lax.axis_index("group")
    owner = [lax.bitwise_xor(me, r) for r in range(groups)]
    where = [chosen[0, owner[r // slots], r % slots] for r in range(rows)]
    column = jnp.concatenate([column_of(where, rows, jnp.int32)] * (length // 128), axis=1)
    onehot = jnp.where(column == lax.broadcasted_iota(jnp.int32, (rows, length), 1), 1.0, 0.0).astype(
        jnp.bfloat16
    )
    live = []
    for r in range(rows):
        e, c = owner[r // slots], r % slots
        live.append(jnp.where(c < counts[0, e], gates[0, e, c], jnp.float32(0.0)))
    scale = jnp.concatenate([column_of(live, rows, jnp.float32)] * (width // 128), axis=1)
    lane = lax.rem(lax.broadcasted_iota(jnp.int32, (8, 2 * rows), 1), rows)
    line = jnp.full((8, 2 * rows), -1, jnp.int32)
    for r in range(rows):
        line = jnp.where(lane == r, where[r], line)
    line = jnp.concatenate([line] * (length // 8), axis=0)
    spot[...] = jnp.where(
        line == lax.broadcasted_iota(jnp.int32, (length, 2 * rows), 0), 1.0, 0.0
    ).astype(jnp.bfloat16)

    for i in range(tiles):
        some = slice(i * width, (i + 1) * width)
        loads[2 * i].wait()
        x = jnp.dot(onehot, tokens[:, some], preferred_element_type=jnp.float32).astype(jnp.bfloat16)
        loads[2 * i + 1].wait()
        g = jnp.dot(onehot, grads[:, some], preferred_element_type=jnp.float32)
        g = (g * scale).astype(jnp.bfloat16)
        for j, out in enumerate(outs):
            d = j % groups
            out[:slots, some] = x[d * slots : (d + 1) * slots]
            out[slots:, some] = g[d * slots : (d + 1) * slots]


def pick(tokens, grads, chosen, counts, gates, groups):
    slots = chosen.shape[2]
    length, model = tokens.shape
    tiles = max(1, model // 512)
    rows = groups * slots
    return pl.pallas_call(
        functools.partial(pick_kernel, groups, slots, tiles),
        in_specs=[anywhere()] * 5,
        out_specs=[vmem()] * (2 * groups + 1),
        out_shape=[jax.ShapeDtypeStruct((2 * slots, model), jnp.bfloat16)] * (2 * groups)
        + [jax.ShapeDtypeStruct((length, 2 * rows), jnp.bfloat16)],
        scratch_shapes=[
            pltpu.SMEM(chosen.shape, chosen.dtype),
            pltpu.SMEM(counts.shape, counts.dtype),
            pltpu.SMEM(gates.shape, gates.dtype),
            pltpu.VMEM((length, model), jnp.bfloat16),
            pltpu.VMEM((length, model), jnp.bfloat16),
            pltpu.SemaphoreType.DMA((3,)),
            pltpu.SemaphoreType.DMA((2 * tiles,)),
        ],
        compiler_params=params(60 * 2**20),
        cost_estimate=cost(4 * rows * length * model, 4 * length * model),
        name="pick",
    )(chosen, counts, gates, tokens, grads)


def vmem():
    return pl.BlockSpec(memory_space=pltpu.VMEM)


def anywhere():
    return pl.BlockSpec(memory_space=pl.ANY)


def join_kernel(n, *refs):
    out = refs[-1]
    at = 0
    for ref in refs[:n]:
        out[at : at + ref.shape[0]] = ref[...]
        at += ref.shape[0]


def join(ins, after):
    rows, model = sum(r.shape[0] for r in ins), ins[0].shape[1]
    return pl.pallas_call(
        functools.partial(join_kernel, len(ins)),
        in_specs=[vmem()] * len(ins) + [anywhere()] * len(after),
        out_specs=vmem(),
        out_shape=jax.ShapeDtypeStruct((rows, model), jnp.bfloat16),
        compiler_params=params(10 * 2**20),
        cost_estimate=cost(0, 4 * rows * model),
        name="join",
    )(*ins, *after)


def block_kernel(slots, tile, n_in, *refs):
    ins, (w_in, w_out) = refs[:n_in], refs[n_in : n_in + 2]
    x_t, act_t, hgrad, g_all, mine, theirs, x_all, g_t, total = refs[-9:]
    half = mine.shape[0]
    at = 0
    for ref in ins:
        for row in range(0, ref.shape[0], 2 * slots):
            x_all[at : at + slots] = ref[row : row + slots]
            g_all[at : at + slots] = ref[row + slots : row + 2 * slots]
            at += slots
    x_t[...] = x_all[...].T
    g_t[...] = g_all[...].T
    for unit in range(0, w_in.shape[2], tile):
        some = slice(unit, unit + tile)
        hidden = jnp.dot(x_all[...], w_in[0, :, some], preferred_element_type=jnp.float32).T
        activation, gelu_slope = gelu_parts(hidden)
        act_t[some] = activation.astype(jnp.bfloat16)
        back = jnp.dot(w_out[0, some], g_t[...], preferred_element_type=jnp.float32)
        hg_t = (back * gelu_slope).astype(jnp.bfloat16)
        hgrad[:, some] = hg_t.T
        part = jnp.dot(w_in[0, :, some], hg_t, preferred_element_type=jnp.float32)
        if unit == 0:
            total[...] = part
        else:
            total[...] += part
    slot_grad = total[...].T
    mine[...] = slot_grad[:half]
    theirs[...] = slot_grad[half:].astype(theirs.dtype)


def block(ins, w_in, w_out, slots, after):
    model, units = w_in.shape[1:]
    rows = sum(r.shape[0] for r in ins) // 2
    half = rows // 2
    bf = functools.partial(jax.ShapeDtypeStruct, dtype=jnp.bfloat16)
    return pl.pallas_call(
        functools.partial(block_kernel, slots, min(256, units), len(ins)),
        in_specs=[vmem()] * (len(ins) + 2) + [anywhere()] * len(after),
        out_specs=[vmem()] * 6,
        out_shape=[
            bf((model, rows)),
            bf((units, rows)),
            bf((rows, units)),
            bf((rows, model)),
            jax.ShapeDtypeStruct((half, model), jnp.float32),
            bf((half, model)),
        ],
        scratch_shapes=[
            pltpu.VMEM((rows, model), jnp.bfloat16),
            pltpu.VMEM((model, rows), jnp.bfloat16),
            pltpu.VMEM((model, rows), jnp.float32),
        ],
        compiler_params=params(20 * 2**20),
        cost_estimate=cost(6 * rows * model * units, 4 * model * units, rows * units),
        name="block",
    )(*ins, w_in, w_out, *after)


def outer_kernel(n, tiles, *refs):
    left_t, right = refs[:n], refs[n : 2 * n]
    out, buf, sems = refs[-3:]
    b = jnp.concatenate([r[...] for r in right], axis=0)
    size = buf.shape[0] // tiles
    copies = []
    for i in range(tiles):
        some = slice(i * size, (i + 1) * size)
        a = jnp.concatenate([r[some] for r in left_t], axis=1)
        buf[some] = jnp.dot(a, b, preferred_element_type=jnp.float32)
        copies.append(pltpu.make_async_copy(buf.at[some], out.at[0, some], sems.at[i]))
        copies[-1].start()
    for copy in copies:
        copy.wait()


def outer(left_ts, rights, after, name):
    n, m, k = len(rights), left_ts[0].shape[0], rights[0].shape[1]
    rows = sum(r.shape[0] for r in rights)
    tiles = 4
    return pl.pallas_call(
        functools.partial(outer_kernel, n, tiles),
        in_specs=[vmem()] * (2 * n) + [anywhere()] * len(after),
        out_specs=anywhere(),
        out_shape=jax.ShapeDtypeStruct((1, m, k), jnp.float32),
        scratch_shapes=[pltpu.VMEM((m, k), jnp.float32), pltpu.SemaphoreType.DMA((tiles,))],
        compiler_params=params(20 * 2**20),
        cost_estimate=cost(2 * rows * m * k, 4 * m * k),
        name=name,
    )(*left_ts, *rights, *after)


def add_kernel(n_in, at, rows, *refs):
    ins, outs = refs[:n_in], refs[n_in:]
    total = None
    for ref in ins:
        part = (ref[...] if ref.shape[0] == rows else ref[at : at + rows]).astype(jnp.float32)
        total = part if total is None else total + part
    total = total.astype(jnp.bfloat16)
    at = 0
    for out in outs:
        out[...] = total[at : at + out.shape[0]]
        at += out.shape[0]


def add_up(ins, cuts, at=0):
    rows, model = sum(cuts), ins[0].shape[1]
    return pl.pallas_call(
        functools.partial(add_kernel, len(ins), at, rows),
        in_specs=[vmem()] * len(ins),
        out_specs=[vmem()] * len(cuts),
        out_shape=[jax.ShapeDtypeStruct((c, model), jnp.bfloat16) for c in cuts],
        compiler_params=params(10 * 2**20),
        cost_estimate=cost(rows * model, 12 * rows * model),
        name="add_up",
    )(*ins)


def place_kernel(tiles, spot, *rest):
    parts, (out, buf, sems) = rest[:-3], rest[-3:]
    values = jnp.concatenate([p[...] for p in parts], axis=0)
    size = buf.shape[0] // tiles
    copies = []
    for i in range(tiles):
        some = slice(i * size, (i + 1) * size)
        buf[some] = jnp.dot(spot[some], values, preferred_element_type=jnp.float32).astype(jnp.bfloat16)
        copies.append(pltpu.make_async_copy(buf.at[some], out.at[some], sems.at[i]))
        copies[-1].start()
    for copy in copies:
        copy.wait()


def place(parts, spot):
    model = parts[0].shape[1]
    length, rows = spot.shape
    tiles = 4
    return pl.pallas_call(
        functools.partial(place_kernel, tiles),
        in_specs=[vmem()] * (1 + len(parts)),
        out_specs=anywhere(),
        out_shape=jax.ShapeDtypeStruct((length, model), jnp.bfloat16),
        scratch_shapes=[pltpu.VMEM((length, model), jnp.bfloat16), pltpu.SemaphoreType.DMA((tiles,))],
        compiler_params=params(10 * 2**20),
        cost_estimate=cost(2 * rows * length * model, 2 * length * model),
        name="place",
    )(spot, *parts)


def shards(tokens_in, out_grad, w_in, w_out, chosen, counts, gates):
    groups = lax.axis_size("group")
    fsdp = lax.axis_size("fsdp")
    ring_len = fsdp // 2
    slots = chosen.shape[2]

    def send(x, group_step, to):
        pairs = [
            (g * fsdp + f, (g ^ group_step) * fsdp + to(f)) for g in range(groups) for f in range(fsdp)
        ]
        return lax.ppermute(x, both, pairs)

    places = [0] + list(range(1, ring_len, 2)) + list(range(2, ring_len, 2))[::-1]
    onward = {p: places[(i + 1) % ring_len] for i, p in enumerate(places)}

    def next_chip(f):
        return 2 * onward[f // 2] + f % 2

    def ring(x):
        return lax.ppermute(x, "fsdp", [(f, next_chip(f)) for f in range(fsdp)])

    def back(x):
        return lax.ppermute(x, "fsdp", [(next_chip(f), f) for f in range(fsdp)])

    def pair(x):
        return lax.ppermute(x, "fsdp", [(f, f ^ 1) for f in range(fsdp)])

    *picked, spot = pick(tokens_in, out_grad, chosen, counts, gates, groups)
    rows = groups * slots
    near = [picked[0]] + [send(picked[d], d, lambda f: f) for d in range(1, groups)]
    ours = join([send(picked[groups + d], d, next_chip) for d in range(groups)], [])
    results, arrived, before = [], [], []
    for k in range(1, ring_len):
        last = k == ring_len - 1
        ahead = None if last else ring(ours)
        mixed = [ours, first, pair(ours), pair(first)] if k == 2 else [ours, pair(ours)]
        results.append(block(mixed, w_in, w_out, slots, before))
        mine, theirs = results[-1][4:]
        total = [mine, pair(theirs)]
        pieces = add_up(total + arrived, [slots] * groups if last else [rows])
        if k == 1:
            returned = back(pieces[0])
            first = join(near, [theirs])
        elif not last:
            arrived = [ring(pieces[0])]
        if k == 2:
            own = add_up(total + [returned], [slots] * groups, rows)
        before = pieces[:1]
        if not last:
            ours = join([ahead], [theirs] + ([first] if k == 1 else []))
    parts = [own[0]] + [send(own[d], d, lambda f: f) for d in range(1, groups)]
    parts += [send(pieces[d], d, next_chip) for d in range(groups)]

    x_ts, act_ts, hgrads, gs = list(zip(*results))[:4]
    grad_w_out = outer(act_ts, gs, [], "grad_w_out")
    grad_w_in = outer(x_ts, hgrads, pieces[:1], "grad_w_in")
    return place(parts, spot), grad_w_in, grad_w_out


def solution(mesh):
    placed = (
        P(("group", "fsdp"), None),
        P(("group", "fsdp"), None),
        P("group", None, "fsdp"),
        P("group", "fsdp", None),
        P(("group", "fsdp"), None, None),
        P(("group", "fsdp"), None),
        P(("group", "fsdp"), None, None),
    )
    return jax.shard_map(
        shards,
        mesh=mesh,
        in_specs=placed,
        out_specs=(P(("group", "fsdp"), None), P("group", None, "fsdp"), P("group", "fsdp", None)),
        check_vma=False,
    )
```

```python
import functools

import jax
import jax.numpy as jnp
from jax import lax
from jax.experimental import pallas as pl
from jax.experimental.pallas import tpu as pltpu
from jax.sharding import PartitionSpec as P

gelu_coef = 0.7978845608028654
both = ("group", "fsdp")


def gelu_parts(hidden):
    inner_arg = gelu_coef * (hidden + 0.044715 * hidden * hidden * hidden)
    tangent = jnp.tanh(inner_arg)
    activation = 0.5 * hidden * (1.0 + tangent)
    slope = 0.5 * (1.0 + tangent) + 0.5 * hidden * (1.0 - tangent * tangent) * gelu_coef * (
        1.0 + 3.0 * 0.044715 * hidden * hidden
    )
    return (activation, slope)


def params(limit=48 * 2**20):
    return pltpu.CompilerParams(vmem_limit_bytes=limit)


def cost(flops, moved, trans=0):
    return pl.CostEstimate(flops=flops, bytes_accessed=moved, transcendentals=trans)


def column_of(values, rows, dtype):
    at = lax.broadcasted_iota(jnp.int32, (8, 128), 0)
    tiles = []
    for base in range(0, rows, 8):
        tile = jnp.full((8, 128), values[base], dtype)
        for r in range(1, 8):
            tile = jnp.where(at == r, values[base + r], tile)
        tiles.append(tile)
    return jnp.concatenate(tiles, axis=0)


def pick_kernel(groups, slots, tiles, chosen_in, counts_in, gates_in, tokens_in, grads_in, *rest):
    outs, spot = rest[: 2 * groups], rest[2 * groups]
    chosen, counts, gates, tokens, grads, small, big = rest[2 * groups + 1 :]
    length, model = tokens.shape
    rows = groups * slots
    width = model // tiles
    scalars = [
        pltpu.make_async_copy(src, dst, small.at[i])
        for i, (src, dst) in enumerate(((chosen_in, chosen), (counts_in, counts), (gates_in, gates)))
    ]
    loads = []
    for i in range(tiles):
        some = slice(i * width, (i + 1) * width)
        for j, (src, dst) in enumerate(((tokens_in, tokens), (grads_in, grads))):
            loads.append(pltpu.make_async_copy(src.at[:, some], dst.at[:, some], big.at[2 * i + j]))
    for copy in scalars + loads:
        copy.start()
    for copy in scalars:
        copy.wait()

    me = lax.axis_index("group")
    owner = [lax.bitwise_xor(me, r) for r in range(groups)]
    where = [chosen[0, owner[r // slots], r % slots] for r in range(rows)]
    column = jnp.concatenate([column_of(where, rows, jnp.int32)] * (length // 128), axis=1)
    onehot = jnp.where(column == lax.broadcasted_iota(jnp.int32, (rows, length), 1), 1.0, 0.0).astype(
        jnp.bfloat16
    )
    live = []
    for r in range(rows):
        e, c = owner[r // slots], r % slots
        live.append(jnp.where(c < counts[0, e], gates[0, e, c], jnp.float32(0.0)))
    scale = jnp.concatenate([column_of(live, rows, jnp.float32)] * (width // 128), axis=1)
    lane = lax.rem(lax.broadcasted_iota(jnp.int32, (8, 2 * rows), 1), rows)
    line = jnp.full((8, 2 * rows), -1, jnp.int32)
    for r in range(rows):
        line = jnp.where(lane == r, where[r], line)
    line = jnp.concatenate([line] * (length // 8), axis=0)
    spot[...] = jnp.where(
        line == lax.broadcasted_iota(jnp.int32, (length, 2 * rows), 0), 1.0, 0.0
    ).astype(jnp.bfloat16)

    for i in range(tiles):
        some = slice(i * width, (i + 1) * width)
        loads[2 * i].wait()
        x = jnp.dot(onehot, tokens[:, some], preferred_element_type=jnp.float32).astype(jnp.bfloat16)
        loads[2 * i + 1].wait()
        g = jnp.dot(onehot, grads[:, some], preferred_element_type=jnp.float32)
        g = (g * scale).astype(jnp.bfloat16)
        for j, out in enumerate(outs):
            d = j % groups
            out[:slots, some] = x[d * slots : (d + 1) * slots]
            out[slots:, some] = g[d * slots : (d + 1) * slots]


def pick(tokens, grads, chosen, counts, gates, groups):
    slots = chosen.shape[2]
    length, model = tokens.shape
    tiles = max(1, model // 512)
    rows = groups * slots
    return pl.pallas_call(
        functools.partial(pick_kernel, groups, slots, tiles),
        in_specs=[anywhere()] * 5,
        out_specs=[vmem()] * (2 * groups + 1),
        out_shape=[jax.ShapeDtypeStruct((2 * slots, model), jnp.bfloat16)] * (2 * groups)
        + [jax.ShapeDtypeStruct((length, 2 * rows), jnp.bfloat16)],
        scratch_shapes=[
            pltpu.SMEM(chosen.shape, chosen.dtype),
            pltpu.SMEM(counts.shape, counts.dtype),
            pltpu.SMEM(gates.shape, gates.dtype),
            pltpu.VMEM((length, model), jnp.bfloat16),
            pltpu.VMEM((length, model), jnp.bfloat16),
            pltpu.SemaphoreType.DMA((3,)),
            pltpu.SemaphoreType.DMA((2 * tiles,)),
        ],
        compiler_params=params(60 * 2**20),
        cost_estimate=cost(4 * rows * length * model, 4 * length * model),
        name="pick",
    )(chosen, counts, gates, tokens, grads)


def vmem():
    return pl.BlockSpec(memory_space=pltpu.VMEM)


def anywhere():
    return pl.BlockSpec(memory_space=pl.ANY)


def join_kernel(n, *refs):
    out = refs[-1]
    at = 0
    for ref in refs[:n]:
        out[at : at + ref.shape[0]] = ref[...]
        at += ref.shape[0]


def join(ins, after):
    rows, model = sum(r.shape[0] for r in ins), ins[0].shape[1]
    return pl.pallas_call(
        functools.partial(join_kernel, len(ins)),
        in_specs=[vmem()] * len(ins) + [anywhere()] * len(after),
        out_specs=vmem(),
        out_shape=jax.ShapeDtypeStruct((rows, model), jnp.bfloat16),
        compiler_params=params(10 * 2**20),
        cost_estimate=cost(0, 4 * rows * model),
        name="join",
    )(*ins, *after)


def block_kernel(slots, tile, n_in, *refs):
    ins, (w_in, w_out) = refs[:n_in], refs[n_in : n_in + 2]
    x_all, act_t, hgrad, g_all, mine, theirs, g_t, total = refs[-8:]
    half = mine.shape[0]
    at = 0
    for ref in ins:
        for row in range(0, ref.shape[0], 2 * slots):
            x_all[at : at + slots] = ref[row : row + slots]
            g_all[at : at + slots] = ref[row + slots : row + 2 * slots]
            at += slots
    g_t[...] = g_all[...].T
    for unit in range(0, w_in.shape[2], tile):
        some = slice(unit, unit + tile)
        hidden = jnp.dot(x_all[...], w_in[0, :, some], preferred_element_type=jnp.float32).T
        activation, gelu_slope = gelu_parts(hidden)
        act_t[some] = activation.astype(jnp.bfloat16)
        back = jnp.dot(w_out[0, some], g_t[...], preferred_element_type=jnp.float32)
        hg_t = (back * gelu_slope).astype(jnp.bfloat16)
        hgrad[:, some] = hg_t.T
        part = jnp.dot(w_in[0, :, some], hg_t, preferred_element_type=jnp.float32)
        if unit == 0:
            total[...] = part
        else:
            total[...] += part
    slot_grad = total[...].T
    mine[...] = slot_grad[:half]
    theirs[...] = slot_grad[half:].astype(theirs.dtype)


def block(ins, w_in, w_out, slots, after):
    model, units = w_in.shape[1:]
    rows = sum(r.shape[0] for r in ins) // 2
    half = rows // 2
    bf = functools.partial(jax.ShapeDtypeStruct, dtype=jnp.bfloat16)
    return pl.pallas_call(
        functools.partial(block_kernel, slots, min(256, units), len(ins)),
        in_specs=[vmem()] * (len(ins) + 2) + [anywhere()] * len(after),
        out_specs=[vmem()] * 6,
        out_shape=[
            bf((rows, model)),
            bf((units, rows)),
            bf((rows, units)),
            bf((rows, model)),
            jax.ShapeDtypeStruct((half, model), jnp.float32),
            bf((half, model)),
        ],
        scratch_shapes=[
            pltpu.VMEM((model, rows), jnp.bfloat16),
            pltpu.VMEM((model, rows), jnp.float32),
        ],
        compiler_params=params(20 * 2**20),
        cost_estimate=cost(3 * rows * model * units, 2 * model * units, rows * units),
        name="block",
    )(*ins, w_in, w_out, *after)


def outer_kernel(n, tiles, turn, *refs):
    left, right = refs[:n], refs[n : 2 * n]
    out, buf, sems = refs[-3:]
    b = jnp.concatenate([r[...] for r in right], axis=0)
    size = buf.shape[0] // tiles
    copies = []
    for i in range(tiles):
        some = slice(i * size, (i + 1) * size)
        a = jnp.concatenate([r[:, some].T if turn else r[some] for r in left], axis=1)
        buf[some] = jnp.dot(a, b, preferred_element_type=jnp.float32)
        copies.append(pltpu.make_async_copy(buf.at[some], out.at[0, some], sems.at[i]))
        copies[-1].start()
    for copy in copies:
        copy.wait()


def outer(lefts, rights, after, turn, name):
    n, m, k = len(rights), lefts[0].shape[1 if turn else 0], rights[0].shape[1]
    rows = sum(r.shape[0] for r in rights)
    tiles = 8
    return pl.pallas_call(
        functools.partial(outer_kernel, n, tiles, turn),
        in_specs=[vmem()] * (2 * n) + [anywhere()] * len(after),
        out_specs=anywhere(),
        out_shape=jax.ShapeDtypeStruct((1, m, k), jnp.float32),
        scratch_shapes=[pltpu.VMEM((m, k), jnp.float32), pltpu.SemaphoreType.DMA((tiles,))],
        compiler_params=params(20 * 2**20),
        cost_estimate=cost(2 * rows * m * k, 4 * m * k),
        name=name,
    )(*lefts, *rights, *after)


def add_kernel(n_in, at, rows, *refs):
    ins, outs = refs[:n_in], refs[n_in:]
    total = None
    for ref in ins:
        part = (ref[...] if ref.shape[0] == rows else ref[at : at + rows]).astype(jnp.float32)
        total = part if total is None else total + part
    total = total.astype(jnp.bfloat16)
    at = 0
    for out in outs:
        out[...] = total[at : at + out.shape[0]]
        at += out.shape[0]


def add_up(ins, cuts, at=0):
    rows, model = sum(cuts), ins[0].shape[1]
    return pl.pallas_call(
        functools.partial(add_kernel, len(ins), at, rows),
        in_specs=[vmem()] * len(ins),
        out_specs=[vmem()] * len(cuts),
        out_shape=[jax.ShapeDtypeStruct((c, model), jnp.bfloat16) for c in cuts],
        compiler_params=params(10 * 2**20),
        cost_estimate=cost(rows * model, 12 * rows * model),
        name="add_up",
    )(*ins)


def place_kernel(tiles, spot, *rest):
    parts, (out, buf, sems) = rest[:-3], rest[-3:]
    values = jnp.concatenate([p[...] for p in parts], axis=0)
    size = buf.shape[0] // tiles
    copies = []
    for i in range(tiles):
        some = slice(i * size, (i + 1) * size)
        buf[some] = jnp.dot(spot[some], values, preferred_element_type=jnp.float32).astype(jnp.bfloat16)
        copies.append(pltpu.make_async_copy(buf.at[some], out.at[some], sems.at[i]))
        copies[-1].start()
    for copy in copies:
        copy.wait()


def place(parts, spot):
    model = parts[0].shape[1]
    length, rows = spot.shape
    tiles = 8
    return pl.pallas_call(
        functools.partial(place_kernel, tiles),
        in_specs=[vmem()] * (1 + len(parts)),
        out_specs=anywhere(),
        out_shape=jax.ShapeDtypeStruct((length, model), jnp.bfloat16),
        scratch_shapes=[pltpu.VMEM((length, model), jnp.bfloat16), pltpu.SemaphoreType.DMA((tiles,))],
        compiler_params=params(10 * 2**20),
        cost_estimate=cost(2 * rows * length * model, 2 * length * model),
        name="place",
    )(spot, *parts)


def shards(tokens_in, out_grad, w_in, w_out, chosen, counts, gates):
    groups = lax.axis_size("group")
    fsdp = lax.axis_size("fsdp")
    ring_len = fsdp // 2
    slots = chosen.shape[2]

    def send(x, group_step, to):
        pairs = [
            (g * fsdp + f, (g ^ group_step) * fsdp + to(f)) for g in range(groups) for f in range(fsdp)
        ]
        return lax.ppermute(x, both, pairs)

    places = [0] + list(range(1, ring_len, 2)) + list(range(2, ring_len, 2))[::-1]
    onward = {p: places[(i + 1) % ring_len] for i, p in enumerate(places)}

    def next_chip(f):
        return 2 * onward[f // 2] + f % 2

    def ring(x):
        return lax.ppermute(x, "fsdp", [(f, next_chip(f)) for f in range(fsdp)])

    def back(x):
        return lax.ppermute(x, "fsdp", [(next_chip(f), f) for f in range(fsdp)])

    def pair(x):
        return lax.ppermute(x, "fsdp", [(f, f ^ 1) for f in range(fsdp)])

    *picked, spot = pick(tokens_in, out_grad, chosen, counts, gates, groups)
    rows = groups * slots
    near = [picked[0]] + [send(picked[d], d, lambda f: f) for d in range(1, groups)]
    ours = join([send(picked[groups + d], d, next_chip) for d in range(groups)], [])
    results, arrived, before = [], [], []
    for k in range(1, ring_len):
        last = k == ring_len - 1
        ahead = None if last else ring(ours)
        mixed = [ours, first, pair(ours), pair(first)] if k == 2 else [ours, pair(ours)]
        results.append(block(mixed, w_in, w_out, slots, before))
        mine, theirs = results[-1][4:]
        total = [mine, pair(theirs)]
        pieces = add_up(total + arrived, [slots] * groups if last else [rows])
        if k == 1:
            returned = back(pieces[0])
            first = join(near, [theirs])
        elif not last:
            arrived = [ring(pieces[0])]
        if k == 2:
            own = add_up(total + [returned], [slots] * groups, rows)
        before = pieces[:1]
        if not last:
            ours = join([ahead], [theirs] + ([first] if k == 1 else []))
    parts = [own[0]] + [send(own[d], d, lambda f: f) for d in range(1, groups)]
    parts += [send(pieces[d], d, next_chip) for d in range(groups)]

    xs, act_ts, hgrads, gs = list(zip(*results))[:4]
    grad_w_out = outer(act_ts, gs, [], False, "grad_w_out")
    grad_w_in = outer(xs, hgrads, pieces[:1], True, "grad_w_in")
    return place(parts, spot), grad_w_in, grad_w_out


def solution(mesh):
    placed = (
        P(("group", "fsdp"), None),
        P(("group", "fsdp"), None),
        P("group", None, "fsdp"),
        P("group", "fsdp", None),
        P(("group", "fsdp"), None, None),
        P(("group", "fsdp"), None),
        P(("group", "fsdp"), None, None),
    )
    return jax.shard_map(
        shards,
        mesh=mesh,
        in_specs=placed,
        out_specs=(P(("group", "fsdp"), None), P("group", None, "fsdp"), P("group", "fsdp", None)),
        check_vma=False,
    )
```

```python
import functools

import jax
import jax.numpy as jnp
from jax import lax
from jax.experimental import pallas as pl
from jax.experimental.pallas import tpu as pltpu
from jax.sharding import PartitionSpec as P

gelu_coef = 0.7978845608028654
both = ("group", "fsdp")


def gelu_parts(hidden):
    inner_arg = gelu_coef * (hidden + 0.044715 * hidden * hidden * hidden)
    tangent = jnp.tanh(inner_arg)
    activation = 0.5 * hidden * (1.0 + tangent)
    slope = 0.5 * (1.0 + tangent) + 0.5 * hidden * (1.0 - tangent * tangent) * gelu_coef * (
        1.0 + 3.0 * 0.044715 * hidden * hidden
    )
    return (activation, slope)


def params(limit=48 * 2**20):
    return pltpu.CompilerParams(vmem_limit_bytes=limit)


def cost(flops, moved, trans=0):
    return pl.CostEstimate(flops=flops, bytes_accessed=moved, transcendentals=trans)


def column_of(values, rows, dtype):
    at = lax.broadcasted_iota(jnp.int32, (8, 128), 0)
    tiles = []
    for base in range(0, rows, 8):
        tile = jnp.full((8, 128), values[base], dtype)
        for r in range(1, 8):
            tile = jnp.where(at == r, values[base + r], tile)
        tiles.append(tile)
    return jnp.concatenate(tiles, axis=0)


def pick_kernel(groups, slots, tiles, chosen_in, counts_in, gates_in, tokens_in, grads_in, *rest):
    outs, spot = rest[: 2 * groups], rest[2 * groups]
    chosen, counts, gates, tokens, grads, small, big = rest[2 * groups + 1 :]
    length, model = tokens.shape
    rows = groups * slots
    width = model // tiles
    scalars = [
        pltpu.make_async_copy(src, dst, small.at[i])
        for i, (src, dst) in enumerate(((chosen_in, chosen), (counts_in, counts), (gates_in, gates)))
    ]
    loads = []
    for i in range(tiles):
        some = slice(i * width, (i + 1) * width)
        for j, (src, dst) in enumerate(((tokens_in, tokens), (grads_in, grads))):
            loads.append(pltpu.make_async_copy(src.at[:, some], dst.at[:, some], big.at[2 * i + j]))
    for copy in scalars + loads:
        copy.start()
    for copy in scalars:
        copy.wait()

    me = lax.axis_index("group")
    owner = [lax.bitwise_xor(me, r) for r in range(groups)]
    where = [chosen[0, owner[r // slots], r % slots] for r in range(rows)]
    column = jnp.concatenate([column_of(where, rows, jnp.int32)] * (length // 128), axis=1)
    onehot = jnp.where(column == lax.broadcasted_iota(jnp.int32, (rows, length), 1), 1.0, 0.0).astype(
        jnp.bfloat16
    )
    live = []
    for r in range(rows):
        e, c = owner[r // slots], r % slots
        live.append(jnp.where(c < counts[0, e], gates[0, e, c], jnp.float32(0.0)))
    scale = jnp.concatenate([column_of(live, rows, jnp.float32)] * (width // 128), axis=1)
    lane = lax.rem(lax.broadcasted_iota(jnp.int32, (8, 2 * rows), 1), rows)
    line = jnp.full((8, 2 * rows), -1, jnp.int32)
    for r in range(rows):
        line = jnp.where(lane == r, where[r], line)
    line = jnp.concatenate([line] * (length // 8), axis=0)
    spot[...] = jnp.where(
        line == lax.broadcasted_iota(jnp.int32, (length, 2 * rows), 0), 1.0, 0.0
    ).astype(jnp.bfloat16)

    for i in range(tiles):
        some = slice(i * width, (i + 1) * width)
        loads[2 * i].wait()
        x = jnp.dot(onehot, tokens[:, some], preferred_element_type=jnp.float32).astype(jnp.bfloat16)
        loads[2 * i + 1].wait()
        g = jnp.dot(onehot, grads[:, some], preferred_element_type=jnp.float32)
        g = (g * scale).astype(jnp.bfloat16)
        for j, out in enumerate(outs):
            d = j % groups
            out[:slots, some] = x[d * slots : (d + 1) * slots]
            out[slots:, some] = g[d * slots : (d + 1) * slots]


def pick(tokens, grads, chosen, counts, gates, groups):
    slots = chosen.shape[2]
    length, model = tokens.shape
    tiles = max(1, model // 512)
    rows = groups * slots
    return pl.pallas_call(
        functools.partial(pick_kernel, groups, slots, tiles),
        in_specs=[anywhere()] * 5,
        out_specs=[vmem()] * (2 * groups + 1),
        out_shape=[jax.ShapeDtypeStruct((2 * slots, model), jnp.bfloat16)] * (2 * groups)
        + [jax.ShapeDtypeStruct((length, 2 * rows), jnp.bfloat16)],
        scratch_shapes=[
            pltpu.SMEM(chosen.shape, chosen.dtype),
            pltpu.SMEM(counts.shape, counts.dtype),
            pltpu.SMEM(gates.shape, gates.dtype),
            pltpu.VMEM((length, model), jnp.bfloat16),
            pltpu.VMEM((length, model), jnp.bfloat16),
            pltpu.SemaphoreType.DMA((3,)),
            pltpu.SemaphoreType.DMA((2 * tiles,)),
        ],
        compiler_params=params(60 * 2**20),
        cost_estimate=cost(4 * rows * length * model, 4 * length * model),
        name="pick",
    )(chosen, counts, gates, tokens, grads)


def vmem():
    return pl.BlockSpec(memory_space=pltpu.VMEM)


def anywhere():
    return pl.BlockSpec(memory_space=pl.ANY)


def join_kernel(n, *refs):
    out = refs[-1]
    at = 0
    for ref in refs[:n]:
        out[at : at + ref.shape[0]] = ref[...]
        at += ref.shape[0]


def join(ins, after):
    rows, model = sum(r.shape[0] for r in ins), ins[0].shape[1]
    return pl.pallas_call(
        functools.partial(join_kernel, len(ins)),
        in_specs=[vmem()] * len(ins) + [anywhere()] * len(after),
        out_specs=vmem(),
        out_shape=jax.ShapeDtypeStruct((rows, model), jnp.bfloat16),
        compiler_params=params(10 * 2**20),
        cost_estimate=cost(0, 4 * rows * model),
        name="join",
    )(*ins, *after)


def block_kernel(slots, tile, n_in, *refs):
    ins, (w_in, w_out) = refs[:n_in], refs[n_in : n_in + 2]
    x_all, act_t, hgrad, g_all, mine, theirs, g_t, total = refs[-8:]
    half = mine.shape[0]
    at = 0
    for ref in ins:
        for row in range(0, ref.shape[0], 2 * slots):
            x_all[at : at + slots] = ref[row : row + slots]
            g_all[at : at + slots] = ref[row + slots : row + 2 * slots]
            at += slots
    g_t[...] = g_all[...].T
    for unit in range(0, w_in.shape[2], tile):
        some = slice(unit, unit + tile)
        hidden = jnp.dot(x_all[...], w_in[0, :, some], preferred_element_type=jnp.float32).T
        activation, gelu_slope = gelu_parts(hidden)
        act_t[some] = activation.astype(jnp.bfloat16)
        back = jnp.dot(w_out[0, some], g_t[...], preferred_element_type=jnp.float32)
        hg_t = (back * gelu_slope).astype(jnp.bfloat16)
        hgrad[:, some] = hg_t.T
        part = jnp.dot(w_in[0, :, some], hg_t, preferred_element_type=jnp.float32)
        if unit == 0:
            total[...] = part
        else:
            total[...] += part
    slot_grad = total[...].T
    mine[...] = slot_grad[:half]
    theirs[...] = slot_grad[half:].astype(theirs.dtype)


def block(ins, w_in, w_out, slots, after):
    model, units = w_in.shape[1:]
    rows = sum(r.shape[0] for r in ins) // 2
    half = rows // 2
    bf = functools.partial(jax.ShapeDtypeStruct, dtype=jnp.bfloat16)
    return pl.pallas_call(
        functools.partial(block_kernel, slots, min(256, units), len(ins)),
        in_specs=[vmem()] * (len(ins) + 2) + [anywhere()] * len(after),
        out_specs=[vmem()] * 6,
        out_shape=[
            bf((rows, model)),
            bf((units, rows)),
            bf((rows, units)),
            bf((rows, model)),
            jax.ShapeDtypeStruct((half, model), jnp.float32),
            bf((half, model)),
        ],
        scratch_shapes=[
            pltpu.VMEM((model, rows), jnp.bfloat16),
            pltpu.VMEM((model, rows), jnp.float32),
        ],
        compiler_params=params(20 * 2**20),
        cost_estimate=cost(3 * rows * model * units, 2 * model * units, rows * units),
        name="block",
    )(*ins, w_in, w_out, *after)


def outer_kernel(n, tiles, turn, *refs):
    left, right = refs[:n], refs[n : 2 * n]
    out, buf, sems = refs[-3:]
    b = jnp.concatenate([r[...] for r in right], axis=0)
    size = buf.shape[0] // tiles
    copies = []
    for i in range(tiles):
        some = slice(i * size, (i + 1) * size)
        a = jnp.concatenate([r[:, some].T if turn else r[some] for r in left], axis=1)
        buf[some] = jnp.dot(a, b, preferred_element_type=jnp.float32)
        copies.append(pltpu.make_async_copy(buf.at[some], out.at[0, some], sems.at[i]))
        copies[-1].start()
    for copy in copies:
        copy.wait()


def outer(lefts, rights, after, turn, name):
    n, m, k = len(rights), lefts[0].shape[1 if turn else 0], rights[0].shape[1]
    rows = sum(r.shape[0] for r in rights)
    tiles = 8
    return pl.pallas_call(
        functools.partial(outer_kernel, n, tiles, turn),
        in_specs=[vmem()] * (2 * n) + [anywhere()] * len(after),
        out_specs=anywhere(),
        out_shape=jax.ShapeDtypeStruct((1, m, k), jnp.float32),
        scratch_shapes=[pltpu.VMEM((m, k), jnp.float32), pltpu.SemaphoreType.DMA((tiles,))],
        compiler_params=params(20 * 2**20),
        cost_estimate=cost(2 * rows * m * k, 4 * m * k),
        name=name,
    )(*lefts, *rights, *after)


def add_kernel(n_in, at, rows, *refs):
    ins, outs = refs[:n_in], refs[n_in:]
    total = None
    for ref in ins:
        part = (ref[...] if ref.shape[0] == rows else ref[at : at + rows]).astype(jnp.float32)
        total = part if total is None else total + part
    total = total.astype(jnp.bfloat16)
    at = 0
    for out in outs:
        out[...] = total[at : at + out.shape[0]]
        at += out.shape[0]


def add_up(ins, cuts, at=0):
    rows, model = sum(cuts), ins[0].shape[1]
    return pl.pallas_call(
        functools.partial(add_kernel, len(ins), at, rows),
        in_specs=[vmem()] * len(ins),
        out_specs=[vmem()] * len(cuts),
        out_shape=[jax.ShapeDtypeStruct((c, model), jnp.bfloat16) for c in cuts],
        compiler_params=params(10 * 2**20),
        cost_estimate=cost(rows * model, 12 * rows * model),
        name="add_up",
    )(*ins)


def place_kernel(tiles, spot, *rest):
    parts, (out, buf, sems) = rest[:-3], rest[-3:]
    values = jnp.concatenate([p[...] for p in parts], axis=0)
    size = buf.shape[0] // tiles
    copies = []
    for i in range(tiles):
        some = slice(i * size, (i + 1) * size)
        buf[some] = jnp.dot(spot[some], values, preferred_element_type=jnp.float32).astype(jnp.bfloat16)
        copies.append(pltpu.make_async_copy(buf.at[some], out.at[some], sems.at[i]))
        copies[-1].start()
    for copy in copies:
        copy.wait()


def place(parts, spot):
    model = parts[0].shape[1]
    length, rows = spot.shape
    tiles = 8
    return pl.pallas_call(
        functools.partial(place_kernel, tiles),
        in_specs=[vmem()] * (1 + len(parts)),
        out_specs=anywhere(),
        out_shape=jax.ShapeDtypeStruct((length, model), jnp.bfloat16),
        scratch_shapes=[pltpu.VMEM((length, model), jnp.bfloat16), pltpu.SemaphoreType.DMA((tiles,))],
        compiler_params=params(10 * 2**20),
        cost_estimate=cost(2 * rows * length * model, 2 * length * model),
        name="place",
    )(spot, *parts)


def shards(tokens_in, out_grad, w_in, w_out, chosen, counts, gates):
    groups = lax.axis_size("group")
    fsdp = lax.axis_size("fsdp")
    ring_len = fsdp // 2
    slots = chosen.shape[2]

    def send(x, group_step, to):
        pairs = [
            (g * fsdp + f, (g ^ group_step) * fsdp + to(f)) for g in range(groups) for f in range(fsdp)
        ]
        return lax.ppermute(x, both, pairs)

    places = [0] + list(range(1, ring_len, 2)) + list(range(2, ring_len, 2))[::-1]
    onward = {p: places[(i + 1) % ring_len] for i, p in enumerate(places)}

    def next_chip(f):
        return 2 * onward[f // 2] + f % 2

    def ring(x):
        return lax.ppermute(x, "fsdp", [(f, next_chip(f)) for f in range(fsdp)])

    def back(x):
        return lax.ppermute(x, "fsdp", [(next_chip(f), f) for f in range(fsdp)])

    def pair(x):
        return lax.ppermute(x, "fsdp", [(f, f ^ 1) for f in range(fsdp)])

    *picked, spot = pick(tokens_in, out_grad, chosen, counts, gates, groups)
    rows = groups * slots
    near = [picked[0]] + [send(picked[d], d, lambda f: f) for d in range(1, groups)]
    ours = join([send(picked[groups + d], d, next_chip) for d in range(groups)], [])
    results, arrived, before = [], [], []
    for k in range(1, ring_len):
        last = k == ring_len - 1
        ahead = None if last else ring(ours)
        mixed = [ours, first, pair(ours), pair(first)] if k == 2 else [ours, pair(ours)]
        results.append(block(mixed, w_in, w_out, slots, before))
        mine, theirs = results[-1][4:]
        total = [mine, pair(theirs)]
        pieces = add_up(total + arrived, [slots] * groups if last else [rows])
        if k == 1:
            returned = back(pieces[0])
            first = join(near, [theirs])
        elif not last:
            arrived = [ring(pieces[0])]
        if k == 2:
            own = add_up(total + [returned], [slots] * groups, rows)
        before = pieces[:1]
        if not last:
            ours = join([ahead], [theirs] + ([first] if k == 1 else []))
    parts = [own[0]] + [send(own[d], d, lambda f: f) for d in range(1, groups)]
    parts += [send(pieces[d], d, next_chip) for d in range(groups - 1, -1, -1)][::-1]

    xs, act_ts, hgrads, gs = list(zip(*results))[:4]
    grad_w_out = outer(act_ts, gs, [], False, "grad_w_out")
    grad_w_in = outer(xs, hgrads, pieces[:1], True, "grad_w_in")
    return place(parts, spot), grad_w_in, grad_w_out


def solution(mesh):
    placed = (
        P(("group", "fsdp"), None),
        P(("group", "fsdp"), None),
        P("group", None, "fsdp"),
        P("group", "fsdp", None),
        P(("group", "fsdp"), None, None),
        P(("group", "fsdp"), None),
        P(("group", "fsdp"), None, None),
    )
    return jax.shard_map(
        shards,
        mesh=mesh,
        in_specs=placed,
        out_specs=(P(("group", "fsdp"), None), P("group", None, "fsdp"), P("group", "fsdp", None)),
        check_vma=False,
    )
```
